32 devices in a mesh: wedge: 4 (over y, x), box: 8 (over z, core).
Axes of the slice: x: 2, y: 2, z: 4, core: 2. Of those that a mesh axis runs over, the one named last changes fastest.
Arguments:
- densities: bfloat16 [256, 4, 128], P('box', 'wedge'), may hold values from -6 to 6
- up_ops: bfloat16 [96, 128, 128], replicated, may hold values from -0.5 to 0.5
- trans_ops: bfloat16 [16, 128, 128], replicated, may hold values from -0.125 to 0.125
- down_ops: bfloat16 [96, 128, 128], replicated, may hold values from -0.0546875 to 0.0546875
- read_table: int32 [8, 128], P('box'), may hold values from 0 to 255, as said below
- interaction: int32 [256, 96, 16], P('box', 'wedge'), may hold values from 0 to 127
Outputs:
- potentials: bfloat16 [256, 4, 128], P('box', 'wedge')
The draws below stay inside these ranges and needn't reach their ends.
Inputs may be any that keep to these rules, and one draw needn't show every extreme that they name: `read_table`: row r holds, for each box group o in order, 16 distinct boxes owned by box group o, numbered o * 32 to o * 32 + 31. interaction[b, w, k] indexes row b // 32 of read_table.
All inputs are finite; a program needn't handle non-finite values.
Results may differ from the reference program's by a relative error of at most 0.0057.
Values may be sent and summed in bfloat16 or wider, within the bound.
A program may use at most 128 MiB of HBM per device.

```python
import math
import jax
import jax.numpy as jnp
from jax import lax

W = 96
C = 128
P_SIZE = 128
F = 4
LIST = 16
BOX_DEV = 32
BOXES = 256
READS = 128
CAP = 16
N_BOX = 8


def draw_read_table(key, part):
    scores = jax.random.randint(key, (N_BOX, N_BOX, BOX_DEV), 0, 1 << 20) * BOX_DEV
    scores = scores + jnp.arange(BOX_DEV, dtype=jnp.int32)
    ordered = jnp.argsort(scores, axis=-1)[:, :, :CAP].astype(jnp.int32)
    owners = jnp.arange(N_BOX, dtype=jnp.int32)[None, :, None] * BOX_DEV
    return (ordered + owners).reshape(N_BOX, READS).astype(jnp.int32)


def place_ends(result, own_key, least, high):
    longest = result.shape.index(max(result.shape))
    spots = []
    for shift in (0, 1):
        where = [jax.random.randint(jax.random.fold_in(own_key, axis), (), 0, length) for axis, length in enumerate(result.shape)]
        where[longest] = (where[longest] + shift) % result.shape[longest]
        spots.append(tuple(where))
    return result.at[spots[0]].set(least).at[spots[1]].set(high)


def block_scale(key, extent, split, low, top_value):
    def one(position, shards_of):
        draws = jax.random.uniform(jax.random.fold_in(jax.random.fold_in(key, 6), position), (shards_of,), jnp.float32, low / len(split), top_value / len(split))
        return jnp.repeat(jnp.exp(draws), extent[position] // shards_of).reshape((-1,) + (1,) * (len(extent) - position - 1))

    loudness = one(*split[0])
    for cut in split[1:]:
        loudness = loudness * one(*cut)
    return loudness


def gaussian(own_key, dims, scale, limit, shards=(), kind=jnp.bfloat16):
    result = jax.random.normal(own_key, dims, jnp.float32) * scale
    if len(shards) > 0:
        result = block_scale(own_key, dims, shards, -0.22, 0.18) * result
    return jnp.clip(result, min=-limit, max=limit).astype(kind)


def setup_inputs(seed: int = 0) -> dict:
    key_of = jax.random.split(jax.random.key(seed), 7)
    return {
        "densities": gaussian(key_of[0], (BOXES, F, P_SIZE), 1.0, 6.0, ((0, 8), (1, 4))),
        "up_ops": gaussian(key_of[1], (W, C, P_SIZE), P_SIZE ** -0.5, 0.5),
        "trans_ops": gaussian(key_of[2], (LIST, C, C), (C * LIST) ** -0.5, 0.125),
        "down_ops": gaussian(key_of[3], (W, P_SIZE, C), (W * C) ** -0.5, 0.0546875),
        "read_table": draw_read_table(jax.random.fold_in(key_of[6], 71), 0),
        "interaction": place_ends(jax.random.randint(key_of[5], (BOXES, W, LIST), 0, READS), jax.random.fold_in(key_of[5], 1), 0, READS - 1).astype(jnp.int32),
    }


def reference(densities, up_ops, trans_ops, down_ops, read_table, interaction):
    group = (jnp.arange(BOXES) // BOX_DEV).astype(jnp.int32)
    source_all = read_table[group[:, None, None], interaction]
    dens_wide = densities.astype(jnp.float32)
    trans_wide = trans_ops.astype(jnp.float32)
    block = math.gcd(BOXES, 512)
    starts = jnp.arange(0, BOXES, block).astype(jnp.int32)

    def wedge_step(carry, wedge_at):
        up_here = lax.dynamic_index_in_dim(up_ops, wedge_at, 0, keepdims=False).astype(jnp.float32)
        down_here = lax.dynamic_index_in_dim(down_ops, wedge_at, 0, keepdims=False).astype(jnp.float32)
        equivalents = jnp.einsum("bfp,cp->bfc", dens_wide, up_here).astype(jnp.bfloat16)
        source_here = lax.dynamic_index_in_dim(source_all, wedge_at, 1, keepdims=False)

        def one_block(start):
            chosen = lax.dynamic_slice_in_dim(source_here, start, block, 0)
            picked = equivalents[chosen].astype(jnp.float32)
            return jnp.einsum("bkfc,kdc->bfd", picked, trans_wide).astype(jnp.bfloat16)

        local_here = lax.map(one_block, starts).reshape(BOXES, F, C)
        carry = carry + jnp.einsum("bfc,pc->bfp", local_here.astype(jnp.float32), down_here)
        return carry, None

    initial = jnp.zeros((BOXES, F, P_SIZE), jnp.float32)
    summed, _ = lax.scan(wedge_step, initial, jnp.arange(W).astype(jnp.int32))
    return summed.astype(jnp.bfloat16)
```

```python
import functools

import jax
import jax.numpy as jnp
from jax import lax
from jax.experimental import pallas as pl
from jax.experimental.pallas import tpu as pltpu
from jax.sharding import PartitionSpec as P

MESH = pl.DeviceIdType.MESH
F32 = jnp.float32
BF16 = jnp.bfloat16


def kernel(
    wedge_groups, box_groups, list_len, group,
    dens_ref, up_ref, trans_ref, down_ref, table_ref, inter_ref, out_ref,
    up_in, trans_in, down_in, table_in, inter_in,
    all_boxes, slots, up_t, trans_t, down_t, select, picked, equiv, total, arrived,
    load_sem, box_send, box_recv, slot_send, slot_recv, part_send, part_recv,
):
    boxes, points = dens_ref.shape
    wedges, coeffs = up_in.shape[0], up_in.shape[1]
    reads = table_ref.shape[1]
    fields = wedge_groups
    me_w = lax.axis_index("wedge")
    me_b = lax.axis_index("box")
    first = me_w * wedges
    my_rows = pl.ds(pl.multiple_of(me_b * boxes, boxes), boxes)

    loads = [
        pltpu.make_async_copy(dens_ref, all_boxes.at[my_rows], load_sem.at[0]),
        pltpu.make_async_copy(table_ref, table_in, load_sem.at[1]),
        pltpu.make_async_copy(inter_ref, inter_in, load_sem.at[2]),
        pltpu.make_async_copy(trans_ref, trans_in, load_sem.at[3]),
        pltpu.make_async_copy(up_ref.at[pl.ds(first, wedges)], up_in, load_sem.at[4]),
        pltpu.make_async_copy(down_ref.at[pl.ds(first, wedges)], down_in, load_sem.at[5]),
    ]

    barrier = pltpu.get_barrier_semaphore()
    for off in range(1, box_groups):
        pl.semaphore_signal(
            barrier, inc=1, device_id={"box": lax.rem(me_b + off, box_groups)}, device_id_type=MESH
        )
    for off in range(1, wedge_groups):
        pl.semaphore_signal(
            barrier, inc=1, device_id={"wedge": lax.rem(me_w + off, wedge_groups)}, device_id_type=MESH
        )
    for load in loads:
        load.start()
    pl.semaphore_wait(barrier, box_groups + wedge_groups - 2)

    box_copies = []
    for off in range(1, box_groups):
        copy = pltpu.make_async_remote_copy(
            src_ref=dens_ref,
            dst_ref=all_boxes.at[my_rows],
            send_sem=box_send.at[off],
            recv_sem=box_recv.at[off],
            device_id={"box": lax.rem(me_b + off, box_groups)},
            device_id_type=MESH,
        )
        copy.start()
        box_copies.append(copy)

    loads[1].wait()
    loads[2].wait()
    lanes = lax.broadcasted_iota(jnp.int32, (boxes, reads), 1)
    per_chunk = 128 // list_len

    def build(chunk, carry):
        rows = inter_in[pl.ds(pl.multiple_of(chunk * 128, 128), 128), :]
        columns = rows.T
        for j in range(per_chunk):
            for k in range(list_len):
                at = j * list_len + k
                hot = (columns[:, at:at + 1] == lanes).astype(F32).astype(BF16)
                select[chunk * per_chunk + j, k * boxes:(k + 1) * boxes, :] = hot
        return carry

    lax.fori_loop(0, wedges // per_chunk, build, 0)

    table_col = jnp.broadcast_to(table_in[...], (reads, reads)).T
    own = lax.broadcasted_iota(jnp.int32, (reads, reads), 1)

    loads[0].wait()
    for off in range(1, box_groups):
        source = lax.rem(me_b - off + box_groups, box_groups)
        rows = pl.ds(pl.multiple_of(source * boxes, boxes), boxes)
        pltpu.make_async_remote_copy(
            src_ref=dens_ref,
            dst_ref=all_boxes.at[rows],
            send_sem=box_send.at[off],
            recv_sem=box_recv.at[off],
            device_id={"box": source},
            device_id_type=MESH,
        ).wait_recv()

    chosen = jnp.zeros((reads, points), F32)
    for tile in range(all_boxes.shape[0] // reads):
        hot = (table_col == own + tile * reads).astype(F32).astype(BF16)
        chosen = chosen + jnp.dot(
            hot, all_boxes[tile * reads:(tile + 1) * reads, :], preferred_element_type=F32
        )
    slots[me_w] = chosen.astype(BF16)

    slot_copies = []
    for off in range(1, wedge_groups):
        copy = pltpu.make_async_remote_copy(
            src_ref=slots.at[me_w],
            dst_ref=slots.at[me_w],
            send_sem=slot_send.at[off],
            recv_sem=slot_recv.at[off],
            device_id={"wedge": lax.rem(me_w + off, wedge_groups)},
            device_id_type=MESH,
        )
        copy.start()
        slot_copies.append(copy)

    for load in loads[3:]:
        load.wait()

    def turn_trans(k, carry):
        trans_t[pl.ds(pl.multiple_of(k * coeffs, coeffs), coeffs), :] = trans_in[k].T
        return carry

    lax.fori_loop(0, list_len, turn_trans, 0)

    def turn_maps(pair, carry):
        for half in range(2):
            w = 2 * pair + half
            up_t[pair, :, half * coeffs:(half + 1) * coeffs] = up_in[w].T
            down_t[pl.ds(pl.multiple_of(w * coeffs, coeffs), coeffs), :] = down_in[w].T
        return carry

    lax.fori_loop(0, wedges // 2, turn_maps, 0)

    total[...] = jnp.zeros_like(total)
    for off in range(1, wedge_groups):
        source = lax.rem(me_w - off + wedge_groups, wedge_groups)
        pltpu.make_async_remote_copy(
            src_ref=slots.at[source],
            dst_ref=slots.at[source],
            send_sem=slot_send.at[off],
            recv_sem=slot_recv.at[off],
            device_id={"wedge": source},
            device_id_type=MESH,
        ).wait_recv()

    def work(step, carry):
        all_slots = slots[...].reshape(fields * reads, points)
        for pair in range(group // 2):
            both = jnp.dot(
                all_slots, up_t[step * (group // 2) + pair], preferred_element_type=F32
            ).astype(BF16)
            for half in range(2):
                for f in range(fields):
                    equiv[2 * pair + half, :, f * coeffs:(f + 1) * coeffs] = both[
                        f * reads:(f + 1) * reads, half * coeffs:(half + 1) * coeffs
                    ]
        for i in range(group):
            got = jnp.dot(
                select[step * group + i], equiv[i], preferred_element_type=F32
            ).astype(BF16)
            for k in range(list_len):
                for f in range(fields):
                    row = (i * fields + f) * boxes
                    picked[row:row + boxes, k * coeffs:(k + 1) * coeffs] = got[
                        k * boxes:(k + 1) * boxes, f * coeffs:(f + 1) * coeffs
                    ]
        local = jnp.dot(picked[...], trans_t[...], preferred_element_type=F32).astype(BF16)
        rows = fields * boxes
        wide = jnp.concatenate([local[i * rows:(i + 1) * rows] for i in range(group)], axis=1)
        span = group * coeffs
        total[...] += jnp.dot(
            wide, down_t[pl.ds(pl.multiple_of(step * span, span), span), :],
            preferred_element_type=F32,
        )
        return carry

    lax.fori_loop(0, wedges // group, work, 0)

    part_copies = []
    for off in range(1, wedge_groups):
        peer = lax.rem(me_w + off, wedge_groups)
        copy = pltpu.make_async_remote_copy(
            src_ref=total.at[pl.ds(pl.multiple_of(peer * boxes, boxes), boxes)],
            dst_ref=arrived.at[off - 1],
            send_sem=part_send.at[off],
            recv_sem=part_recv.at[off],
            device_id={"wedge": peer},
            device_id_type=MESH,
        )
        copy.start()
        part_copies.append(copy)
    for copy in box_copies + slot_copies:
        copy.wait_send()
    result = total[pl.ds(pl.multiple_of(me_w * boxes, boxes), boxes), :]
    for off, copy in enumerate(part_copies):
        copy.wait_recv()
        result = result + arrived[off]
    out_ref[...] = result.astype(BF16)
    for copy in part_copies:
        copy.wait_send()


def body(densities, up_ops, trans_ops, down_ops, read_table, interaction):
    boxes, _, points = densities.shape
    coeffs = up_ops.shape[1]
    wedge_groups = lax.axis_size("wedge")
    box_groups = lax.axis_size("box")
    wedges = up_ops.shape[0] // wedge_groups
    list_len = interaction.shape[2]
    reads = read_table.shape[1]
    fields = wedge_groups
    group = 4
    lists = interaction.transpose(1, 2, 0).reshape(wedges * list_len, boxes)
    anywhere = pl.BlockSpec(memory_space=pl.ANY)
    flops = 2 * wedges * fields * coeffs * (
        reads * points + boxes * list_len * (reads + coeffs) + boxes * points
    )
    result = pl.pallas_call(
        functools.partial(kernel, wedge_groups, box_groups, list_len, group),
        out_shape=jax.ShapeDtypeStruct((boxes, points), BF16),
        in_specs=[anywhere] * 6,
        out_specs=pl.BlockSpec(memory_space=pltpu.VMEM),
        scratch_shapes=[
            pltpu.VMEM((wedges, coeffs, points), BF16),
            pltpu.VMEM((list_len, coeffs, coeffs), BF16),
            pltpu.VMEM((wedges, points, coeffs), BF16),
            pltpu.VMEM((1, reads), jnp.int32),
            pltpu.VMEM((wedges * list_len, boxes), jnp.int32),
            pltpu.VMEM((box_groups * boxes, points), BF16),
            pltpu.VMEM((fields, reads, points), BF16),
            pltpu.VMEM((wedges // 2, points, 2 * coeffs), BF16),
            pltpu.VMEM((list_len * coeffs, coeffs), BF16),
            pltpu.VMEM((wedges * coeffs, points), BF16),
            pltpu.VMEM((wedges, list_len * boxes, reads), BF16),
            pltpu.VMEM((group * fields * boxes, list_len * coeffs), BF16),
            pltpu.VMEM((group, reads, fields * coeffs), BF16),
            pltpu.VMEM((fields * boxes, points), F32),
            pltpu.VMEM((wedge_groups - 1, boxes, points), F32),
            pltpu.SemaphoreType.DMA((6,)),
            pltpu.SemaphoreType.DMA((box_groups,)),
            pltpu.SemaphoreType.DMA((box_groups,)),
            pltpu.SemaphoreType.DMA((wedge_groups,)),
            pltpu.SemaphoreType.DMA((wedge_groups,)),
            pltpu.SemaphoreType.DMA((wedge_groups,)),
            pltpu.SemaphoreType.DMA((wedge_groups,)),
        ],
        compiler_params=pltpu.CompilerParams(
            collective_id=0, has_side_effects=True, vmem_limit_bytes=48 * 1024 * 1024
        ),
        cost_estimate=pl.CostEstimate(flops=flops, bytes_accessed=3 << 20, transcendentals=0),
    )(densities.reshape(boxes, points), up_ops, trans_ops, down_ops, read_table, lists)
    return result.reshape(boxes, 1, points)


def solution(mesh):
    in_specs = (P("box", "wedge", None), P(), P(), P(), P("box", None), P("box", "wedge", None))
    out_specs = P("box", "wedge", None)
    return jax.shard_map(body, mesh=mesh, in_specs=in_specs, out_specs=out_specs, check_vma=False)
```

```python
import functools

import jax
import jax.numpy as jnp
from jax import lax
from jax.experimental import pallas as pl
from jax.experimental.pallas import tpu as pltpu
from jax.sharding import PartitionSpec as P

MESH = pl.DeviceIdType.MESH
F32 = jnp.float32
BF16 = jnp.bfloat16


def kernel(
    wedge_groups, box_groups, list_len, group,
    dens_ref, up_ref, trans_ref, down_ref, table_ref, inter_ref, out_ref,
    up_in, trans_in, down_in, table_in, inter_in,
    all_boxes, slots, trans_t, select, picked, equiv, total, arrived,
    load_sem, box_send, box_recv, slot_send, slot_recv, part_send, part_recv,
):
    boxes, points = dens_ref.shape
    wedges, coeffs = up_in.shape[0], up_in.shape[1]
    reads = table_ref.shape[1]
    fields = wedge_groups
    me_w = lax.axis_index("wedge")
    me_b = lax.axis_index("box")
    first = me_w * wedges
    my_rows = pl.ds(pl.multiple_of(me_b * boxes, boxes), boxes)

    loads = [
        pltpu.make_async_copy(dens_ref, all_boxes.at[my_rows], load_sem.at[0]),
        pltpu.make_async_copy(table_ref, table_in, load_sem.at[1]),
        pltpu.make_async_copy(inter_ref, inter_in, load_sem.at[2]),
        pltpu.make_async_copy(trans_ref, trans_in, load_sem.at[3]),
        pltpu.make_async_copy(up_ref.at[pl.ds(first, wedges)], up_in, load_sem.at[4]),
        pltpu.make_async_copy(down_ref.at[pl.ds(first, wedges)], down_in, load_sem.at[5]),
    ]

    barrier = pltpu.get_barrier_semaphore()
    for off in range(1, box_groups):
        pl.semaphore_signal(
            barrier, inc=1, device_id={"box": lax.rem(me_b + off, box_groups)}, device_id_type=MESH
        )
    for off in range(1, wedge_groups):
        pl.semaphore_signal(
            barrier, inc=1, device_id={"wedge": lax.rem(me_w + off, wedge_groups)}, device_id_type=MESH
        )
    for load in loads:
        load.start()
    pl.semaphore_wait(barrier, box_groups + wedge_groups - 2)

    box_copies = []
    for off in range(1, box_groups):
        copy = pltpu.make_async_remote_copy(
            src_ref=dens_ref,
            dst_ref=all_boxes.at[my_rows],
            send_sem=box_send.at[off],
            recv_sem=box_recv.at[off],
            device_id={"box": lax.rem(me_b + off, box_groups)},
            device_id_type=MESH,
        )
        copy.start()
        box_copies.append(copy)

    loads[1].wait()
    loads[2].wait()
    lanes = lax.broadcasted_iota(jnp.int32, (boxes, reads), 1)
    per_chunk = 128 // list_len

    def build(chunk, carry):
        rows = inter_in[pl.ds(pl.multiple_of(chunk * 128, 128), 128), :]
        columns = rows.T
        for j in range(per_chunk):
            for k in range(list_len):
                at = j * list_len + k
                hot = (columns[:, at:at + 1] == lanes).astype(F32).astype(BF16)
                select[chunk * per_chunk + j, k * boxes:(k + 1) * boxes, :] = hot
        return carry

    lax.fori_loop(0, wedges // per_chunk, build, 0)

    table_col = jnp.broadcast_to(table_in[...], (reads, reads)).T
    own = lax.broadcasted_iota(jnp.int32, (reads, reads), 1)

    loads[0].wait()
    for off in range(1, box_groups):
        source = lax.rem(me_b - off + box_groups, box_groups)
        rows = pl.ds(pl.multiple_of(source * boxes, boxes), boxes)
        pltpu.make_async_remote_copy(
            src_ref=dens_ref,
            dst_ref=all_boxes.at[rows],
            send_sem=box_send.at[off],
            recv_sem=box_recv.at[off],
            device_id={"box": source},
            device_id_type=MESH,
        ).wait_recv()

    chosen = jnp.zeros((reads, points), F32)
    for tile in range(all_boxes.shape[0] // reads):
        hot = (table_col == own + tile * reads).astype(F32).astype(BF16)
        chosen = chosen + jnp.dot(
            hot, all_boxes[tile * reads:(tile + 1) * reads, :], preferred_element_type=F32
        )
    slots[me_w] = chosen.astype(BF16)

    slot_copies = []
    for off in range(1, wedge_groups):
        copy = pltpu.make_async_remote_copy(
            src_ref=slots.at[me_w],
            dst_ref=slots.at[me_w],
            send_sem=slot_send.at[off],
            recv_sem=slot_recv.at[off],
            device_id={"wedge": lax.rem(me_w + off, wedge_groups)},
            device_id_type=MESH,
        )
        copy.start()
        slot_copies.append(copy)

    for load in loads[3:]:
        load.wait()

    def turn_trans(k, carry):
        trans_t[pl.ds(pl.multiple_of(k * coeffs, coeffs), coeffs), :] = trans_in[k].T
        return carry

    lax.fori_loop(0, list_len, turn_trans, 0)

    total[...] = jnp.zeros_like(total)
    for off in range(1, wedge_groups):
        source = lax.rem(me_w - off + wedge_groups, wedge_groups)
        pltpu.make_async_remote_copy(
            src_ref=slots.at[source],
            dst_ref=slots.at[source],
            send_sem=slot_send.at[off],
            recv_sem=slot_recv.at[off],
            device_id={"wedge": source},
            device_id_type=MESH,
        ).wait_recv()

    def outgoing(pair, carry):
        all_slots = slots[...].reshape(fields * reads, points)
        maps = up_in[pl.ds(2 * pair, 2)].reshape(2 * coeffs, points)
        both = lax.dot_general(
            all_slots, maps, (((1,), (1,)), ((), ())), preferred_element_type=F32
        ).astype(BF16)
        for half in range(2):
            for f in range(fields):
                equiv[2 * pair + half, :, f * coeffs:(f + 1) * coeffs] = both[
                    f * reads:(f + 1) * reads, half * coeffs:(half + 1) * coeffs
                ]
        return carry

    lax.fori_loop(0, wedges // 2, outgoing, 0)

    def work(step, carry):
        for i in range(group):
            got = jnp.dot(
                select[step * group + i], equiv[step * group + i], preferred_element_type=F32
            ).astype(BF16)
            for k in range(list_len):
                for f in range(fields):
                    row = (i * fields + f) * boxes
                    picked[row:row + boxes, k * coeffs:(k + 1) * coeffs] = got[
                        k * boxes:(k + 1) * boxes, f * coeffs:(f + 1) * coeffs
                    ]
        local = jnp.dot(picked[...], trans_t[...], preferred_element_type=F32).astype(BF16)
        rows = fields * boxes
        wide = jnp.concatenate([local[i * rows:(i + 1) * rows] for i in range(group)], axis=1)
        maps = jnp.concatenate([down_in[step * group + i] for i in range(group)], axis=1)
        total[...] += lax.dot_general(
            wide, maps, (((1,), (1,)), ((), ())), preferred_element_type=F32
        )
        return carry

    lax.fori_loop(0, wedges // group, work, 0)

    part_copies = []
    for off in range(1, wedge_groups):
        peer = lax.rem(me_w + off, wedge_groups)
        copy = pltpu.make_async_remote_copy(
            src_ref=total.at[pl.ds(pl.multiple_of(peer * boxes, boxes), boxes)],
            dst_ref=arrived.at[off - 1],
            send_sem=part_send.at[off],
            recv_sem=part_recv.at[off],
            device_id={"wedge": peer},
            device_id_type=MESH,
        )
        copy.start()
        part_copies.append(copy)
    for copy in box_copies + slot_copies:
        copy.wait_send()
    result = total[pl.ds(pl.multiple_of(me_w * boxes, boxes), boxes), :]
    for off, copy in enumerate(part_copies):
        copy.wait_recv()
        result = result + arrived[off]
    out_ref[...] = result.astype(BF16)
    for copy in part_copies:
        copy.wait_send()


def body(densities, up_ops, trans_ops, down_ops, read_table, interaction):
    boxes, _, points = densities.shape
    coeffs = up_ops.shape[1]
    wedge_groups = lax.axis_size("wedge")
    box_groups = lax.axis_size("box")
    wedges = up_ops.shape[0] // wedge_groups
    list_len = interaction.shape[2]
    reads = read_table.shape[1]
    fields = wedge_groups
    group = 8
    lists = interaction.transpose(1, 2, 0).reshape(wedges * list_len, boxes)
    anywhere = pl.BlockSpec(memory_space=pltpu.HBM)
    flops = 2 * wedges * fields * coeffs * (
        reads * points + boxes * list_len * (reads + coeffs) + boxes * points
    )
    result = pl.pallas_call(
        functools.partial(kernel, wedge_groups, box_groups, list_len, group),
        out_shape=jax.ShapeDtypeStruct((boxes, points), BF16),
        in_specs=[anywhere] * 6,
        out_specs=pl.BlockSpec(memory_space=pltpu.VMEM),
        scratch_shapes=[
            pltpu.VMEM((wedges, coeffs, points), BF16),
            pltpu.VMEM((list_len, coeffs, coeffs), BF16),
            pltpu.VMEM((wedges, points, coeffs), BF16),
            pltpu.VMEM((1, reads), jnp.int32),
            pltpu.VMEM((wedges * list_len, boxes), jnp.int32),
            pltpu.VMEM((box_groups * boxes, points), BF16),
            pltpu.VMEM((fields, reads, points), BF16),
            pltpu.VMEM((list_len * coeffs, coeffs), BF16),
            pltpu.VMEM((wedges, list_len * boxes, reads), BF16),
            pltpu.VMEM((group * fields * boxes, list_len * coeffs), BF16),
            pltpu.VMEM((wedges, reads, fields * coeffs), BF16),
            pltpu.VMEM((fields * boxes, points), F32),
            pltpu.VMEM((wedge_groups - 1, boxes, points), F32),
            pltpu.SemaphoreType.DMA((6,)),
            pltpu.SemaphoreType.DMA((box_groups,)),
            pltpu.SemaphoreType.DMA((box_groups,)),
            pltpu.SemaphoreType.DMA((wedge_groups,)),
            pltpu.SemaphoreType.DMA((wedge_groups,)),
            pltpu.SemaphoreType.DMA((wedge_groups,)),
            pltpu.SemaphoreType.DMA((wedge_groups,)),
        ],
        compiler_params=pltpu.CompilerParams(
            collective_id=0, has_side_effects=True, vmem_limit_bytes=64 * 1024 * 1024
        ),
        cost_estimate=pl.CostEstimate(flops=flops, bytes_accessed=3 << 20, transcendentals=0),
    )(densities.reshape(boxes, points), up_ops, trans_ops, down_ops, read_table, lists)
    return result.reshape(boxes, 1, points)


def solution(mesh):
    in_specs = (P("box", "wedge", None), P(), P(), P(), P("box", None), P("box", "wedge", None))
    out_specs = P("box", "wedge", None)
    return jax.shard_map(body, mesh=mesh, in_specs=in_specs, out_specs=out_specs, check_vma=False)
```

```python
import functools

import jax
import jax.numpy as jnp
from jax import lax
from jax.experimental import pallas as pl
from jax.experimental.pallas import tpu as pltpu
from jax.sharding import PartitionSpec as P

MESH = pl.DeviceIdType.MESH
F32 = jnp.float32
BF16 = jnp.bfloat16


def kernel(
    wedge_groups, box_groups, list_len, group,
    dens_ref, up_ref, trans_ref, down_ref, table_ref, inter_ref, out_ref,
    up_in, trans_in, down_in, table_in, inter_in,
    all_boxes, slots, trans_t, select, even, odd, equiv, total, arrived,
    load_sem, box_send, box_recv, slot_send, slot_recv, part_send, part_recv,
):
    boxes, points = dens_ref.shape
    wedges, coeffs = up_in.shape[0], up_in.shape[1]
    reads = table_ref.shape[1]
    fields = wedge_groups
    me_w = lax.axis_index("wedge")
    me_b = lax.axis_index("box")
    first = me_w * wedges
    my_rows = pl.ds(pl.multiple_of(me_b * boxes, boxes), boxes)

    loads = [
        pltpu.make_async_copy(dens_ref, all_boxes.at[my_rows], load_sem.at[0]),
        pltpu.make_async_copy(table_ref, table_in, load_sem.at[1]),
        pltpu.make_async_copy(inter_ref, inter_in, load_sem.at[2]),
        pltpu.make_async_copy(trans_ref, trans_in, load_sem.at[3]),
        pltpu.make_async_copy(up_ref.at[pl.ds(first, wedges)], up_in, load_sem.at[4]),
        pltpu.make_async_copy(down_ref.at[pl.ds(first, wedges)], down_in, load_sem.at[5]),
    ]

    barrier = pltpu.get_barrier_semaphore()
    for off in range(1, box_groups):
        pl.semaphore_signal(
            barrier, inc=1, device_id={"box": lax.rem(me_b + off, box_groups)}, device_id_type=MESH
        )
    for off in range(1, wedge_groups):
        pl.semaphore_signal(
            barrier, inc=1, device_id={"wedge": lax.rem(me_w + off, wedge_groups)}, device_id_type=MESH
        )
    for load in loads:
        load.start()
    pl.semaphore_wait(barrier, box_groups + wedge_groups - 2)

    box_copies = []
    for off in range(1, box_groups):
        copy = pltpu.make_async_remote_copy(
            src_ref=dens_ref,
            dst_ref=all_boxes.at[my_rows],
            send_sem=box_send.at[off],
            recv_sem=box_recv.at[off],
            device_id={"box": lax.rem(me_b + off, box_groups)},
            device_id_type=MESH,
        )
        copy.start()
        box_copies.append(copy)

    loads[3].wait()

    def turn_trans(k, carry):
        trans_t[pl.ds(pl.multiple_of(k * coeffs, coeffs), coeffs), :] = trans_in[k].T
        return carry

    lax.fori_loop(0, list_len, turn_trans, 0, unroll=4)

    loads[1].wait()
    loads[2].wait()
    lanes = lax.broadcasted_iota(jnp.int32, (boxes, reads), 1)
    per_chunk = 128 // list_len

    def build(chunk, carry):
        rows = inter_in[pl.ds(pl.multiple_of(chunk * 128, 128), 128), :]
        columns = rows.T
        for j in range(per_chunk):
            for k in range(list_len):
                at = j * list_len + k
                hot = (columns[:, at:at + 1] == lanes).astype(F32).astype(BF16)
                select[chunk * per_chunk + j, k * boxes:(k + 1) * boxes, :] = hot
        return carry

    lax.fori_loop(0, 1, build, 0)

    table_col = jnp.broadcast_to(table_in[...], (reads, reads)).T
    own = lax.broadcasted_iota(jnp.int32, (reads, reads), 1)

    loads[0].wait()
    for off in range(1, box_groups):
        source = lax.rem(me_b - off + box_groups, box_groups)
        rows = pl.ds(pl.multiple_of(source * boxes, boxes), boxes)
        pltpu.make_async_remote_copy(
            src_ref=dens_ref,
            dst_ref=all_boxes.at[rows],
            send_sem=box_send.at[off],
            recv_sem=box_recv.at[off],
            device_id={"box": source},
            device_id_type=MESH,
        ).wait_recv()

    chosen = jnp.zeros((reads, points), F32)
    for tile in range(all_boxes.shape[0] // reads):
        hot = (table_col == own + tile * reads).astype(F32).astype(BF16)
        chosen = chosen + jnp.dot(
            hot, all_boxes[tile * reads:(tile + 1) * reads, :], preferred_element_type=F32
        )
    slots[me_w] = chosen.astype(BF16)

    slot_copies = []
    for off in range(1, wedge_groups):
        copy = pltpu.make_async_remote_copy(
            src_ref=slots.at[me_w],
            dst_ref=slots.at[me_w],
            send_sem=slot_send.at[off],
            recv_sem=slot_recv.at[off],
            device_id={"wedge": lax.rem(me_w + off, wedge_groups)},
            device_id_type=MESH,
        )
        copy.start()
        slot_copies.append(copy)

    lax.fori_loop(1, wedges // per_chunk, build, 0)
    loads[4].wait()
    loads[5].wait()

    total[...] = jnp.zeros_like(total)
    for off in range(1, wedge_groups):
        source = lax.rem(me_w - off + wedge_groups, wedge_groups)
        pltpu.make_async_remote_copy(
            src_ref=slots.at[source],
            dst_ref=slots.at[source],
            send_sem=slot_send.at[off],
            recv_sem=slot_recv.at[off],
            device_id={"wedge": source},
            device_id_type=MESH,
        ).wait_recv()

    def outgoing(pair, carry):
        all_slots = slots[...].reshape(fields * reads, points)
        maps = up_in[pl.ds(2 * pair, 2)].reshape(2 * coeffs, points)
        both = lax.dot_general(
            all_slots, maps, (((1,), (1,)), ((), ())), preferred_element_type=F32
        ).astype(BF16)
        for half in range(2):
            for f in range(fields):
                equiv[2 * pair + half, :, f * coeffs:(f + 1) * coeffs] = both[
                    f * reads:(f + 1) * reads, half * coeffs:(half + 1) * coeffs
                ]
        return carry

    lax.fori_loop(0, wedges // 2, outgoing, 0)

    def gather(step, picked):
        for i in range(group):
            got = jnp.dot(
                select[step * group + i], equiv[step * group + i], preferred_element_type=F32
            ).astype(BF16)
            for k in range(list_len):
                for f in range(fields):
                    row = (i * fields + f) * boxes
                    picked[row:row + boxes, k * coeffs:(k + 1) * coeffs] = got[
                        k * boxes:(k + 1) * boxes, f * coeffs:(f + 1) * coeffs
                    ]

    def translate(step, picked):
        local = jnp.dot(picked[...], trans_t[...], preferred_element_type=F32).astype(BF16)
        rows = fields * boxes
        wide = jnp.concatenate([local[i * rows:(i + 1) * rows] for i in range(group)], axis=1)
        maps = jnp.concatenate([down_in[step * group + i] for i in range(group)], axis=1)
        total[...] += lax.dot_general(
            wide, maps, (((1,), (1,)), ((), ())), preferred_element_type=F32
        )

    steps = wedges // group
    gather(0, even)

    def work(turn, carry):
        gather(2 * turn + 1, odd)
        translate(2 * turn, even)
        gather(2 * turn + 2, even)
        translate(2 * turn + 1, odd)
        return carry

    lax.fori_loop(0, steps // 2 - 1, work, 0)
    gather(steps - 1, odd)
    translate(steps - 2, even)
    translate(steps - 1, odd)

    part_copies = []
    for off in range(1, wedge_groups):
        peer = lax.rem(me_w + off, wedge_groups)
        copy = pltpu.make_async_remote_copy(
            src_ref=total.at[pl.ds(pl.multiple_of(peer * boxes, boxes), boxes)],
            dst_ref=arrived.at[off - 1],
            send_sem=part_send.at[off],
            recv_sem=part_recv.at[off],
            device_id={"wedge": peer},
            device_id_type=MESH,
        )
        copy.start()
        part_copies.append(copy)
    for copy in box_copies + slot_copies:
        copy.wait_send()
    result = total[pl.ds(pl.multiple_of(me_w * boxes, boxes), boxes), :]
    for off, copy in enumerate(part_copies):
        copy.wait_recv()
        result = result + arrived[off]
    out_ref[...] = result.astype(BF16)
    for copy in part_copies:
        copy.wait_send()


def body(densities, up_ops, trans_ops, down_ops, read_table, interaction):
    boxes, _, points = densities.shape
    coeffs = up_ops.shape[1]
    wedge_groups = lax.axis_size("wedge")
    box_groups = lax.axis_size("box")
    wedges = up_ops.shape[0] // wedge_groups
    list_len = interaction.shape[2]
    reads = read_table.shape[1]
    fields = wedge_groups
    group = 4
    lists = interaction.transpose(1, 2, 0).reshape(wedges * list_len, boxes)
    anywhere = pl.BlockSpec(memory_space=pltpu.HBM)
    flops = 2 * wedges * fields * coeffs * (
        reads * points + boxes * list_len * (reads + coeffs) + boxes * points
    )
    result = pl.pallas_call(
        functools.partial(kernel, wedge_groups, box_groups, list_len, group),
        out_shape=jax.ShapeDtypeStruct((boxes, points), BF16),
        in_specs=[anywhere] * 6,
        out_specs=pl.BlockSpec(memory_space=pltpu.VMEM),
        scratch_shapes=[
            pltpu.VMEM((wedges, coeffs, points), BF16),
            pltpu.VMEM((list_len, coeffs, coeffs), BF16),
            pltpu.VMEM((wedges, points, coeffs), BF16),
            pltpu.VMEM((1, reads), jnp.int32),
            pltpu.VMEM((wedges * list_len, boxes), jnp.int32),
            pltpu.VMEM((box_groups * boxes, points), BF16),
            pltpu.VMEM((fields, reads, points), BF16),
            pltpu.VMEM((list_len * coeffs, coeffs), BF16),
            pltpu.VMEM((wedges, list_len * boxes, reads), BF16),
            pltpu.VMEM((group * fields * boxes, list_len * coeffs), BF16),
            pltpu.VMEM((group * fields * boxes, list_len * coeffs), BF16),
            pltpu.VMEM((wedges, reads, fields * coeffs), BF16),
            pltpu.VMEM((fields * boxes, points), F32),
            pltpu.VMEM((wedge_groups - 1, boxes, points), F32),
            pltpu.SemaphoreType.DMA((6,)),
            pltpu.SemaphoreType.DMA((box_groups,)),
            pltpu.SemaphoreType.DMA((box_groups,)),
            pltpu.SemaphoreType.DMA((wedge_groups,)),
            pltpu.SemaphoreType.DMA((wedge_groups,)),
            pltpu.SemaphoreType.DMA((wedge_groups,)),
            pltpu.SemaphoreType.DMA((wedge_groups,)),
        ],
        compiler_params=pltpu.CompilerParams(
            collective_id=0, has_side_effects=True, vmem_limit_bytes=64 * 1024 * 1024
        ),
        cost_estimate=pl.CostEstimate(flops=flops, bytes_accessed=3 << 20, transcendentals=0),
    )(densities.reshape(boxes, points), up_ops, trans_ops, down_ops, read_table, lists)
    return result.reshape(boxes, 1, points)


def solution(mesh):
    in_specs = (P("box", "wedge", None), P(), P(), P(), P("box", None), P("box", "wedge", None))
    out_specs = P("box", "wedge", None)
    return jax.shard_map(body, mesh=mesh, in_specs=in_specs, out_specs=out_specs, check_vma=False)
```

```python
import functools

import jax
import jax.numpy as jnp
from jax import lax
from jax.experimental import pallas as pl
from jax.experimental.pallas import tpu as pltpu
from jax.sharding import PartitionSpec as P

MESH = pl.DeviceIdType.MESH
F32 = jnp.float32
BF16 = jnp.bfloat16


def kernel(
    wedge_groups, box_groups, list_len, group,
    dens_ref, up_ref, trans_ref, down_ref, table_ref, inter_ref, out_ref,
    up_in, trans_in, down_in, table_in, inter_in,
    all_boxes, slots, trans_t, select, picked, equiv, total, arrived,
    load_sem, box_send, box_recv, slot_send, slot_recv, part_send, part_recv,
):
    boxes, points = dens_ref.shape
    wedges, coeffs = up_in.shape[0], up_in.shape[1]
    reads = table_ref.shape[1]
    fields = wedge_groups
    me_w = lax.axis_index("wedge")
    me_b = lax.axis_index("box")
    first = me_w * wedges
    my_rows = pl.ds(pl.multiple_of(me_b * boxes, boxes), boxes)

    loads = [
        pltpu.make_async_copy(dens_ref, all_boxes.at[my_rows], load_sem.at[0]),
        pltpu.make_async_copy(table_ref, table_in, load_sem.at[1]),
        pltpu.make_async_copy(inter_ref, inter_in, load_sem.at[2]),
        pltpu.make_async_copy(trans_ref, trans_in, load_sem.at[3]),
        pltpu.make_async_copy(up_ref.at[pl.ds(first, wedges)], up_in, load_sem.at[4]),
        pltpu.make_async_copy(down_ref.at[pl.ds(first, wedges)], down_in, load_sem.at[5]),
    ]

    barrier = pltpu.get_barrier_semaphore()
    for off in range(1, box_groups):
        pl.semaphore_signal(
            barrier, inc=1, device_id={"box": lax.rem(me_b + off, box_groups)}, device_id_type=MESH
        )
    for off in range(1, wedge_groups):
        pl.semaphore_signal(
            barrier, inc=1, device_id={"wedge": lax.rem(me_w + off, wedge_groups)}, device_id_type=MESH
        )
    for load in loads:
        load.start()
    pl.semaphore_wait(barrier, box_groups + wedge_groups - 2)

    box_copies = []
    for off in range(1, box_groups):
        copy = pltpu.make_async_remote_copy(
            src_ref=dens_ref,
            dst_ref=all_boxes.at[my_rows],
            send_sem=box_send.at[off],
            recv_sem=box_recv.at[off],
            device_id={"box": lax.rem(me_b + off, box_groups)},
            device_id_type=MESH,
        )
        copy.start()
        box_copies.append(copy)

    loads[3].wait()

    def turn_trans(k, carry):
        trans_t[pl.ds(pl.multiple_of(k * coeffs, coeffs), coeffs), :] = trans_in[k].T
        return carry

    lax.fori_loop(0, list_len, turn_trans, 0, unroll=2)

    loads[1].wait()
    loads[2].wait()
    lanes = lax.broadcasted_iota(jnp.int32, (boxes, reads), 1)
    early = wedges // 3

    def build(w, carry):
        columns = inter_in[pl.ds(pl.multiple_of(w * list_len, list_len), list_len), :].T
        for k in range(list_len):
            hot = (columns[:, k:k + 1] == lanes).astype(F32).astype(BF16)
            select[w, k * boxes:(k + 1) * boxes, :] = hot
        return carry

    lax.fori_loop(0, early, build, 0)

    table_col = jnp.broadcast_to(table_in[...], (reads, reads)).T
    own = lax.broadcasted_iota(jnp.int32, (reads, reads), 1)

    loads[0].wait()
    for off in range(1, box_groups):
        source = lax.rem(me_b - off + box_groups, box_groups)
        rows = pl.ds(pl.multiple_of(source * boxes, boxes), boxes)
        pltpu.make_async_remote_copy(
            src_ref=dens_ref,
            dst_ref=all_boxes.at[rows],
            send_sem=box_send.at[off],
            recv_sem=box_recv.at[off],
            device_id={"box": source},
            device_id_type=MESH,
        ).wait_recv()

    chosen = jnp.zeros((reads, points), F32)
    for tile in range(all_boxes.shape[0] // reads):
        hot = (table_col == own + tile * reads).astype(F32).astype(BF16)
        chosen = chosen + jnp.dot(
            hot, all_boxes[tile * reads:(tile + 1) * reads, :], preferred_element_type=F32
        )
    slots[me_w] = chosen.astype(BF16)

    slot_copies = []
    for off in range(1, wedge_groups):
        copy = pltpu.make_async_remote_copy(
            src_ref=slots.at[me_w],
            dst_ref=slots.at[me_w],
            send_sem=slot_send.at[off],
            recv_sem=slot_recv.at[off],
            device_id={"wedge": lax.rem(me_w + off, wedge_groups)},
            device_id_type=MESH,
        )
        copy.start()
        slot_copies.append(copy)

    lax.fori_loop(early, wedges, build, 0)
    loads[4].wait()
    loads[5].wait()

    total[...] = jnp.zeros_like(total)
    for off in range(1, wedge_groups):
        source = lax.rem(me_w - off + wedge_groups, wedge_groups)
        pltpu.make_async_remote_copy(
            src_ref=slots.at[source],
            dst_ref=slots.at[source],
            send_sem=slot_send.at[off],
            recv_sem=slot_recv.at[off],
            device_id={"wedge": source},
            device_id_type=MESH,
        ).wait_recv()

    def outgoing(pair, carry):
        all_slots = slots[...].reshape(fields * reads, points)
        maps = up_in[pl.ds(2 * pair, 2)].reshape(2 * coeffs, points)
        both = lax.dot_general(
            all_slots, maps, (((1,), (1,)), ((), ())), preferred_element_type=F32
        ).astype(BF16)
        for half in range(2):
            for f in range(fields):
                equiv[2 * pair + half, :, f * coeffs:(f + 1) * coeffs] = both[
                    f * reads:(f + 1) * reads, half * coeffs:(half + 1) * coeffs
                ]
        return carry

    lax.fori_loop(0, wedges // 2, outgoing, 0)

    def work(step, carry):
        def gather(pair, carry):
            for half in range(2):
                i = 2 * pair + half
                got = jnp.dot(
                    select[step * group + i], equiv[step * group + i], preferred_element_type=F32
                ).astype(BF16)
                for f in range(fields):
                    row = pl.multiple_of((i * fields + f) * boxes, boxes)
                    for k in range(list_len):
                        picked[pl.ds(row, boxes), k * coeffs:(k + 1) * coeffs] = got[
                            k * boxes:(k + 1) * boxes, f * coeffs:(f + 1) * coeffs
                        ]
            return carry

        lax.fori_loop(0, group // 2, gather, 0)
        local = jnp.dot(picked[...], trans_t[...], preferred_element_type=F32).astype(BF16)
        rows = fields * boxes
        wide = jnp.concatenate([local[i * rows:(i + 1) * rows] for i in range(group)], axis=1)
        maps = jnp.concatenate([down_in[step * group + i] for i in range(group)], axis=1)
        total[...] += lax.dot_general(
            wide, maps, (((1,), (1,)), ((), ())), preferred_element_type=F32
        )
        return carry

    lax.fori_loop(0, wedges // group, work, 0)

    part_copies = []
    for off in range(1, wedge_groups):
        peer = lax.rem(me_w + off, wedge_groups)
        copy = pltpu.make_async_remote_copy(
            src_ref=total.at[pl.ds(pl.multiple_of(peer * boxes, boxes), boxes)],
            dst_ref=arrived.at[off - 1],
            send_sem=part_send.at[off],
            recv_sem=part_recv.at[off],
            device_id={"wedge": peer},
            device_id_type=MESH,
        )
        copy.start()
        part_copies.append(copy)
    for copy in box_copies + slot_copies:
        copy.wait_send()
    result = total[pl.ds(pl.multiple_of(me_w * boxes, boxes), boxes), :]
    for off, copy in enumerate(part_copies):
        copy.wait_recv()
        result = result + arrived[off]
    out_ref[...] = result.astype(BF16)
    for copy in part_copies:
        copy.wait_send()


def body(densities, up_ops, trans_ops, down_ops, read_table, interaction):
    boxes, _, points = densities.shape
    coeffs = up_ops.shape[1]
    wedge_groups = lax.axis_size("wedge")
    box_groups = lax.axis_size("box")
    wedges = up_ops.shape[0] // wedge_groups
    list_len = interaction.shape[2]
    reads = read_table.shape[1]
    fields = wedge_groups
    group = 8
    lists = interaction.transpose(1, 2, 0).reshape(wedges * list_len, boxes)
    anywhere = pl.BlockSpec(memory_space=pltpu.HBM)
    flops = 2 * wedges * fields * coeffs * (
        reads * points + boxes * list_len * (reads + coeffs) + boxes * points
    )
    result = pl.pallas_call(
        functools.partial(kernel, wedge_groups, box_groups, list_len, group),
        out_shape=jax.ShapeDtypeStruct((boxes, points), BF16),
        in_specs=[anywhere] * 6,
        out_specs=pl.BlockSpec(memory_space=pltpu.VMEM),
        scratch_shapes=[
            pltpu.VMEM((wedges, coeffs, points), BF16),
            pltpu.VMEM((list_len, coeffs, coeffs), BF16),
            pltpu.VMEM((wedges, points, coeffs), BF16),
            pltpu.VMEM((1, reads), jnp.int32),
            pltpu.VMEM((wedges * list_len, boxes), jnp.int32),
            pltpu.VMEM((box_groups * boxes, points), BF16),
            pltpu.VMEM((fields, reads, points), BF16),
            pltpu.VMEM((list_len * coeffs, coeffs), BF16),
            pltpu.VMEM((wedges, list_len * boxes, reads), BF16),
            pltpu.VMEM((group * fields * boxes, list_len * coeffs), BF16),
            pltpu.VMEM((wedges, reads, fields * coeffs), BF16),
            pltpu.VMEM((fields * boxes, points), F32),
            pltpu.VMEM((wedge_groups - 1, boxes, points), F32),
            pltpu.SemaphoreType.DMA((6,)),
            pltpu.SemaphoreType.DMA((box_groups,)),
            pltpu.SemaphoreType.DMA((box_groups,)),
            pltpu.SemaphoreType.DMA((wedge_groups,)),
            pltpu.SemaphoreType.DMA((wedge_groups,)),
            pltpu.SemaphoreType.DMA((wedge_groups,)),
            pltpu.SemaphoreType.DMA((wedge_groups,)),
        ],
        compiler_params=pltpu.CompilerParams(
            collective_id=0, has_side_effects=True, vmem_limit_bytes=64 * 1024 * 1024
        ),
        cost_estimate=pl.CostEstimate(flops=flops, bytes_accessed=3 << 20, transcendentals=0),
    )(densities.reshape(boxes, points), up_ops, trans_ops, down_ops, read_table, lists)
    return result.reshape(boxes, 1, points)


def solution(mesh):
    in_specs = (P("box", "wedge", None), P(), P(), P(), P("box", None), P("box", "wedge", None))
    out_specs = P("box", "wedge", None)
    return jax.shard_map(body, mesh=mesh, in_specs=in_specs, out_specs=out_specs, check_vma=False)
```

```python
import functools

import jax
import jax.numpy as jnp
from jax import lax
from jax.experimental import pallas as pl
from jax.experimental.pallas import tpu as pltpu
from jax.sharding import PartitionSpec as P

MESH = pl.DeviceIdType.MESH
F32 = jnp.float32
BF16 = jnp.bfloat16


def kernel(
    wedge_groups, box_groups, list_len, group,
    dens_ref, up_ref, trans_ref, down_ref, table_ref, inter_ref, out_ref,
    up_in, trans_in, down_in, table_in, inter_in,
    all_boxes, slots, trans_t, select, picked, equiv, total, arrived,
    load_sem, box_send, box_recv, slot_send, slot_recv, part_send, part_recv,
):
    boxes, points = dens_ref.shape
    wedges, coeffs = up_in.shape[0], up_in.shape[1]
    reads = table_ref.shape[1]
    fields = wedge_groups
    me_w = lax.axis_index("wedge")
    me_b = lax.axis_index("box")
    first = me_w * wedges
    my_rows = pl.ds(pl.multiple_of(me_b * boxes, boxes), boxes)

    loads = [
        pltpu.make_async_copy(dens_ref, all_boxes.at[my_rows], load_sem.at[0]),
        pltpu.make_async_copy(table_ref, table_in, load_sem.at[1]),
        pltpu.make_async_copy(inter_ref, inter_in, load_sem.at[2]),
        pltpu.make_async_copy(trans_ref, trans_in, load_sem.at[3]),
        pltpu.make_async_copy(up_ref.at[pl.ds(first, wedges)], up_in, load_sem.at[4]),
        pltpu.make_async_copy(down_ref.at[pl.ds(first, wedges)], down_in, load_sem.at[5]),
    ]

    barrier = pltpu.get_barrier_semaphore()
    for off in range(1, box_groups):
        pl.semaphore_signal(
            barrier, inc=1, device_id={"box": lax.rem(me_b + off, box_groups)}, device_id_type=MESH
        )
    for off in range(1, wedge_groups):
        pl.semaphore_signal(
            barrier, inc=1, device_id={"wedge": lax.rem(me_w + off, wedge_groups)}, device_id_type=MESH
        )
    for load in loads:
        load.start()
    pl.semaphore_wait(barrier, box_groups + wedge_groups - 2)

    box_copies = []
    for off in range(1, box_groups):
        copy = pltpu.make_async_remote_copy(
            src_ref=dens_ref,
            dst_ref=all_boxes.at[my_rows],
            send_sem=box_send.at[off],
            recv_sem=box_recv.at[off],
            device_id={"box": lax.rem(me_b + off, box_groups)},
            device_id_type=MESH,
        )
        copy.start()
        box_copies.append(copy)

    loads[1].wait()
    loads[2].wait()
    lanes = lax.broadcasted_iota(jnp.int32, (boxes, reads), 1)
    per_chunk = 128 // list_len

    def build(chunk, carry):
        rows = inter_in[pl.ds(pl.multiple_of(chunk * 128, 128), 128), :]
        columns = rows.T
        for j in range(per_chunk):
            for k in range(list_len):
                at = j * list_len + k
                hot = (columns[:, at:at + 1] == lanes).astype(F32).astype(BF16)
                select[chunk * per_chunk + j, k * boxes:(k + 1) * boxes, :] = hot
        return carry

    lax.fori_loop(0, wedges // per_chunk, build, 0)

    table_col = jnp.broadcast_to(table_in[...], (reads, reads)).T
    own = lax.broadcasted_iota(jnp.int32, (reads, reads), 1)

    loads[0].wait()
    for off in range(1, box_groups):
        source = lax.rem(me_b - off + box_groups, box_groups)
        rows = pl.ds(pl.multiple_of(source * boxes, boxes), boxes)
        pltpu.make_async_remote_copy(
            src_ref=dens_ref,
            dst_ref=all_boxes.at[rows],
            send_sem=box_send.at[off],
            recv_sem=box_recv.at[off],
            device_id={"box": source},
            device_id_type=MESH,
        ).wait_recv()

    chosen = jnp.zeros((reads, points), F32)
    for tile in range(all_boxes.shape[0] // reads):
        hot = (table_col == own + tile * reads).astype(F32).astype(BF16)
        chosen = chosen + jnp.dot(
            hot, all_boxes[tile * reads:(tile + 1) * reads, :], preferred_element_type=F32
        )
    slots[me_w] = chosen.astype(BF16)

    slot_copies = []
    for off in range(1, wedge_groups):
        copy = pltpu.make_async_remote_copy(
            src_ref=slots.at[me_w],
            dst_ref=slots.at[me_w],
            send_sem=slot_send.at[off],
            recv_sem=slot_recv.at[off],
            device_id={"wedge": lax.rem(me_w + off, wedge_groups)},
            device_id_type=MESH,
        )
        copy.start()
        slot_copies.append(copy)

    for load in loads[3:]:
        load.wait()

    def turn_trans(k, carry):
        trans_t[pl.ds(pl.multiple_of(k * coeffs, coeffs), coeffs), :] = trans_in[k].T
        return carry

    lax.fori_loop(0, list_len, turn_trans, 0, unroll=8)

    total[...] = jnp.zeros_like(total)
    for off in range(1, wedge_groups):
        source = lax.rem(me_w - off + wedge_groups, wedge_groups)
        pltpu.make_async_remote_copy(
            src_ref=slots.at[source],
            dst_ref=slots.at[source],
            send_sem=slot_send.at[off],
            recv_sem=slot_recv.at[off],
            device_id={"wedge": source},
            device_id_type=MESH,
        ).wait_recv()

    def outgoing(pair, carry):
        all_slots = slots[...].reshape(fields * reads, points)
        maps = up_in[pl.ds(2 * pair, 2)].reshape(2 * coeffs, points)
        both = lax.dot_general(
            all_slots, maps, (((1,), (1,)), ((), ())), preferred_element_type=F32
        ).astype(BF16)
        for half in range(2):
            for f in range(fields):
                equiv[2 * pair + half, :, f * coeffs:(f + 1) * coeffs] = both[
                    f * reads:(f + 1) * reads, half * coeffs:(half + 1) * coeffs
                ]
        return carry

    lax.fori_loop(0, wedges // 2, outgoing, 0, unroll=4)

    def work(step, carry):
        for i in range(group):
            got = jnp.dot(
                select[step * group + i], equiv[step * group + i], preferred_element_type=F32
            ).astype(BF16)
            for k in range(list_len):
                for f in range(fields):
                    row = (i * fields + f) * boxes
                    picked[row:row + boxes, k * coeffs:(k + 1) * coeffs] = got[
                        k * boxes:(k + 1) * boxes, f * coeffs:(f + 1) * coeffs
                    ]
        local = jnp.dot(picked[...], trans_t[...], preferred_element_type=F32).astype(BF16)
        rows = fields * boxes
        wide = jnp.concatenate([local[i * rows:(i + 1) * rows] for i in range(group)], axis=1)
        maps = jnp.concatenate([down_in[step * group + i] for i in range(group)], axis=1)
        total[...] += lax.dot_general(
            wide, maps, (((1,), (1,)), ((), ())), preferred_element_type=F32
        )
        return carry

    lax.fori_loop(0, wedges // group, work, 0)

    part_copies = []
    for off in range(1, wedge_groups):
        peer = lax.rem(me_w + off, wedge_groups)
        copy = pltpu.make_async_remote_copy(
            src_ref=total.at[pl.ds(pl.multiple_of(peer * boxes, boxes), boxes)],
            dst_ref=arrived.at[off - 1],
            send_sem=part_send.at[off],
            recv_sem=part_recv.at[off],
            device_id={"wedge": peer},
            device_id_type=MESH,
        )
        copy.start()
        part_copies.append(copy)
    for copy in box_copies + slot_copies:
        copy.wait_send()
    result = total[pl.ds(pl.multiple_of(me_w * boxes, boxes), boxes), :]
    for off, copy in enumerate(part_copies):
        copy.wait_recv()
        result = result + arrived[off]
    out_ref[...] = result.astype(BF16)
    for copy in part_copies:
        copy.wait_send()


def body(densities, up_ops, trans_ops, down_ops, read_table, interaction):
    boxes, _, points = densities.shape
    coeffs = up_ops.shape[1]
    wedge_groups = lax.axis_size("wedge")
    box_groups = lax.axis_size("box")
    wedges = up_ops.shape[0] // wedge_groups
    list_len = interaction.shape[2]
    reads = read_table.shape[1]
    fields = wedge_groups
    group = 8
    lists = interaction.transpose(1, 2, 0).reshape(wedges * list_len, boxes)
    anywhere = pl.BlockSpec(memory_space=pltpu.HBM)
    flops = 2 * wedges * fields * coeffs * (
        reads * points + boxes * list_len * (reads + coeffs) + boxes * points
    )
    result = pl.pallas_call(
        functools.partial(kernel, wedge_groups, box_groups, list_len, group),
        out_shape=jax.ShapeDtypeStruct((boxes, points), BF16),
        in_specs=[anywhere] * 6,
        out_specs=pl.BlockSpec(memory_space=pltpu.VMEM),
        scratch_shapes=[
            pltpu.VMEM((wedges, coeffs, points), BF16),
            pltpu.VMEM((list_len, coeffs, coeffs), BF16),
            pltpu.VMEM((wedges, points, coeffs), BF16),
            pltpu.VMEM((1, reads), jnp.int32),
            pltpu.VMEM((wedges * list_len, boxes), jnp.int32),
            pltpu.VMEM((box_groups * boxes, points), BF16),
            pltpu.VMEM((fields, reads, points), BF16),
            pltpu.VMEM((list_len * coeffs, coeffs), BF16),
            pltpu.VMEM((wedges, list_len * boxes, reads), BF16),
            pltpu.VMEM((group * fields * boxes, list_len * coeffs), BF16),
            pltpu.VMEM((wedges, reads, fields * coeffs), BF16),
            pltpu.VMEM((fields * boxes, points), F32),
            pltpu.VMEM((wedge_groups - 1, boxes, points), F32),
            pltpu.SemaphoreType.DMA((6,)),
            pltpu.SemaphoreType.DMA((box_groups,)),
            pltpu.SemaphoreType.DMA((box_groups,)),
            pltpu.SemaphoreType.DMA((wedge_groups,)),
            pltpu.SemaphoreType.DMA((wedge_groups,)),
            pltpu.SemaphoreType.DMA((wedge_groups,)),
            pltpu.SemaphoreType.DMA((wedge_groups,)),
        ],
        compiler_params=pltpu.CompilerParams(
            collective_id=0, has_side_effects=True, vmem_limit_bytes=64 * 1024 * 1024
        ),
        cost_estimate=pl.CostEstimate(flops=flops, bytes_accessed=3 << 20, transcendentals=0),
    )(densities.reshape(boxes, points), up_ops, trans_ops, down_ops, read_table, lists)
    return result.reshape(boxes, 1, points)


def solution(mesh):
    in_specs = (P("box", "wedge", None), P(), P(), P(), P("box", None), P("box", "wedge", None))
    out_specs = P("box", "wedge", None)
    return jax.shard_map(body, mesh=mesh, in_specs=in_specs, out_specs=out_specs, check_vma=False)
```
